32 devices in a mesh: groups: 1, row: 16 (over z, y, x), col: 2 (over core).
Axes of the slice: x: 2, y: 2, z: 4, core: 2. Of those that a mesh axis runs over, the one named last changes fastest.
Arguments:
- wave_now: float32 [2, 2048, 4096], P('groups', 'row', 'col'), may hold values from -6 to 6
- wave_before: float32 [2, 2048, 4096], P('groups', 'row', 'col'), may hold values from -6 to 6
- fault_slip: float32 [2048, 4096], P(('groups', 'row'), 'col'), may hold values from 0 to 2
- region_ids: int32 [128, 256], P(('groups', 'row'), 'col'), may hold values from 0 to 7
- mode_history: bfloat16 [16, 2, 4096, 2048], P('groups', None, ('row', 'col')), may hold values from -6 to 6
- wave_kernel: bfloat16 [16, 4096, 2048], P(None, ('row', 'col')), may hold values from -1.5 to 1.5
- static_friction: float32 [8], replicated, may hold values from 0.55 to 0.75
- dynamic_friction: float32 [8], replicated, may hold values from 0.2 to 0.45
- weakening_slip: float32 [8], replicated, may hold values from 0.3 to 3
- normal_stress: float32 [8], replicated, may hold values from 2 to 5
- initial_stress: float32 [8], replicated, may hold values from -1.5 to 1.5
Outputs:
- final_wave: float32 [2, 2048, 4096], P('groups', 'row', 'col')
- final_slip: float32 [2048, 4096], P(('groups', 'row'), 'col')
- fault_traction: float32 [2048, 4096], P(('groups', 'row'), 'col')
The draws below stay inside these ranges and needn't reach their ends.
All inputs are finite; a program needn't handle non-finite values.
Results may differ from the reference program's by a relative error of at most 0.0003.
Values sent between devices are 32-bit elements; how exact they have to be, the bound alone decides.
A program may use at most 128 MiB of HBM per device.

```python
import math
import jax
import jax.numpy as jnp

NX = 2048
NY = 4096
DEPTH = 2
HORIZON = 16
SUBSTEPS = 2
BLOCK_CELLS = 16
REGIONS = 8
REGION_ROWS = 128
REGION_COLS = 256


def place_ends(result, key, low, top_value):
    place = [jax.random.randint(jax.random.fold_in(key, axis), (), 0, length) for axis, length in enumerate(result.shape)]
    widest = result.shape.index(max(result.shape))
    beside = place[:widest] + [(place[widest] + 1) % result.shape[widest]] + place[widest + 1:]
    return result.at[tuple(place)].set(low).at[tuple(beside)].set(top_value)


def level_of(rng, extent, split, least, largest):
    def one(axis_at, parts):
        draws = jax.random.uniform(jax.random.fold_in(jax.random.fold_in(rng, 6), axis_at), (parts,), jnp.float32, least / len(split), largest / len(split))
        return jnp.repeat(jnp.exp(draws), extent[axis_at] // parts).reshape((-1,) + (1,) * (len(extent) - axis_at - 1))

    factor_of = one(*split[0])
    for cut in split[1:]:
        factor_of = factor_of * one(*cut)
    return factor_of


def normal_values(own_key, extent, scale, reach, split=(), held_as=jnp.bfloat16):
    values = scale * jax.random.normal(own_key, extent, jnp.float32)
    if split:
        values = values * level_of(own_key, extent, split, -0.22, 0.18)
    return jnp.clip(values, -reach, reach).astype(held_as)


def setup_inputs(seed: int = 0, part: int = 0) -> dict:
    key_list = jax.random.split(jax.random.key(seed), 12)
    part_splits = jax.random.split(jax.random.fold_in(key_list[11], part), 12)
    wave_now = normal_values(part_splits[0], (DEPTH, NX, NY), 1.0, 6.0, ((1, 16), (2, 2)), jnp.float32)
    wave_before = normal_values(part_splits[1], (DEPTH, NX, NY), 1.0, 6.0, ((1, 16), (2, 2)), jnp.float32)
    fault_slip = jnp.clip(2.0 * jax.random.uniform(part_splits[2], (NX, NY), jnp.float32) ** level_of(part_splits[2], (NX, NY), ((0, 16), (1, 2)), -0.2, 0.2), 0.0, 2.0)
    region_ids = place_ends(jax.random.randint(part_splits[3], (REGION_ROWS, REGION_COLS), 0, REGIONS), jax.random.fold_in(part_splits[3], 1), 0, REGIONS - 1).astype(jnp.int32)
    mode_history = normal_values(part_splits[4], (HORIZON, 2, NY, NX), 1.0, 6.0, ((2, 32),))
    wave_kernel = normal_values(key_list[5], (HORIZON, NY, NX), 0.25, 1.5, ((1, 32),))
    static_friction = jnp.clip(jax.random.uniform(key_list[6], (REGIONS,), jnp.float32, 0.55, 0.75), 0.55, 0.75)
    dynamic_friction = jnp.clip(jax.random.uniform(key_list[7], (REGIONS,), jnp.float32, 0.2, 0.45), 0.2, 0.45)
    weakening_slip = jnp.clip(jnp.exp(jax.random.uniform(key_list[8], (REGIONS,), jnp.float32, math.log(0.3), math.log(3.0))), 0.3, 3.0)
    normal_stress = jnp.clip(jax.random.uniform(key_list[9], (REGIONS,), jnp.float32, 2.0, 5.0), 2.0, 5.0)
    initial_stress = jnp.clip(jax.random.uniform(key_list[10], (REGIONS,), jnp.float32, -1.5, 1.5), -1.5, 1.5)
    return dict(wave_now=wave_now, wave_before=wave_before, fault_slip=fault_slip, region_ids=region_ids, mode_history=mode_history, wave_kernel=wave_kernel, static_friction=static_friction, dynamic_friction=dynamic_friction, weakening_slip=weakening_slip, normal_stress=normal_stress, initial_stress=initial_stress)


damping = 0.5
courant = 0.3


def reference(wave_now, wave_before, fault_slip, region_ids, mode_history, wave_kernel, static_friction, dynamic_friction, weakening_slip, normal_stress, initial_stress):
    cell_ids = jnp.repeat(jnp.repeat(region_ids, BLOCK_CELLS, axis=0), BLOCK_CELLS, axis=1).astype(jnp.int32)
    static_level = static_friction[cell_ids]
    dynamic_level = dynamic_friction[cell_ids]
    weakening = weakening_slip[cell_ids]
    normal_load = normal_stress[cell_ids]
    prestress = initial_stress[cell_ids]
    current = wave_now
    previous = wave_before
    slip = fault_slip
    traction = jnp.zeros_like(fault_slip)
    recent = []
    for substep in range(SUBSTEPS):
        slip_rate = current[0] - previous[0]
        transform = jnp.fft.fft2(slip_rate, norm="ortho").T
        recent.insert(0, jnp.stack([jnp.real(transform), jnp.imag(transform)]).astype(jnp.float32))
        fresh = len(recent)
        wave_load = jnp.zeros((2, NY, NX), jnp.float32)
        for offset in range(fresh):
            wave_load = wave_load + wave_kernel[offset].astype(jnp.float32)[None] * recent[offset]
        for offset in range(fresh, HORIZON):
            wave_load = wave_load + wave_kernel[offset].astype(jnp.float32)[None] * mode_history[offset - fresh].astype(jnp.float32)
        combined = (wave_load[0] + 1j * wave_load[1]).T
        far_field = jnp.real(jnp.fft.ifft2(combined, norm="ortho")).astype(jnp.float32)
        trial_stress = prestress + far_field - damping * slip_rate
        strength = normal_load * (static_level - (static_level - dynamic_level) * jnp.minimum(slip / weakening, 1.0))
        traction = jnp.clip(trial_stress, -strength, strength)
        slip = slip + jnp.abs(slip_rate)
        laplacian = (jnp.roll(current, 1, 1) + jnp.roll(current, -1, 1) + jnp.roll(current, 1, 2) + jnp.roll(current, -1, 2) - 4.0 * current)
        upper_cells = jnp.concatenate([current[1:], jnp.zeros_like(current[:1])], 0)
        lower_cells = jnp.concatenate([(current[0] + traction)[None], current[:-1]], 0)
        following = 2.0 * current - previous + courant * (laplacian + upper_cells + lower_cells - 2.0 * current)
        previous = current
        current = following
    return current, slip, traction
```

```python
import functools
import math

import jax
import jax.numpy as jnp
import numpy as np
from jax import lax
from jax.experimental import pallas as pl
from jax.experimental.pallas import tpu as pltpu
from jax.sharding import PartitionSpec as P

SUBSTEPS = 2
BLOCK_CELLS = 16

damping = 0.5
courant = 0.3
CHUNKS = 2
VMEM_BYTES = 60 * 1024 * 1024
f32 = jnp.float32
bf16 = jnp.bfloat16


def split_table(table):
    table = table.astype(np.float32)
    high = table.astype(bf16)
    low = (table - high.astype(np.float32)).astype(bf16)
    return high, low


def y_table(length, lanes):
    count = length // lanes
    a = np.arange(count, dtype=np.int64)[:, None, None]
    b = np.arange(lanes, dtype=np.int64)[None, :, None]
    q = np.arange(lanes, dtype=np.int64)[None, None, :]
    angle = 2.0 * np.pi / length * (((count * b + a) * q) % length)
    return split_table(np.concatenate([np.cos(angle), -np.sin(angle)], 2) / math.sqrt(length))


def x_table(length, lanes=128):
    count = length // lanes
    a = np.arange(count, dtype=np.int64)[:, None, None]
    b = np.arange(lanes, dtype=np.int64)[None, :, None]
    k = np.arange(lanes, dtype=np.int64)[None, None, :]
    angle = 2.0 * np.pi / length * (((count * b + a) * k) % length)
    cos, sin = np.cos(angle), np.sin(angle)
    top = np.concatenate([cos, -sin], 2)
    low = np.concatenate([sin, cos], 2)
    return split_table(np.concatenate([top, low], 1) / math.sqrt(length))


def fft_list(re, im, sign):
    count = len(re)
    if count == 1:
        return re, im
    ere, eim = fft_list(re[0::2], im[0::2], sign)
    ore, oim = fft_list(re[1::2], im[1::2], sign)
    half = count // 2
    out_re, out_im = [None] * count, [None] * count
    for k in range(half):
        angle = sign * 2.0 * math.pi * k / count
        c, s = math.cos(angle), math.sin(angle)
        if k == 0:
            tre, tim = ore[k], oim[k]
        elif 4 * k == count:
            tre, tim = (-oim[k], ore[k]) if sign > 0 else (oim[k], -ore[k])
        elif 8 * k == count:
            r = math.sqrt(0.5)
            tre, tim = (ore[k] - sign * oim[k]) * r, (oim[k] + sign * ore[k]) * r
        else:
            tre, tim = ore[k] * c - oim[k] * s, ore[k] * s + oim[k] * c
        out_re[k], out_im[k] = ere[k] + tre, eim[k] + tim
        out_re[k + half], out_im[k + half] = ere[k] - tre, eim[k] - tim
    return out_re, out_im


def halves(values):
    high = values.astype(bf16)
    return high, (values - high.astype(f32)).astype(bf16)


def dot_nn(values, high, low):
    vh, vl = halves(values)
    dot = functools.partial(jnp.dot, preferred_element_type=f32)
    return dot(vh, high) + (dot(vl, high) + dot(vh, low))


def dot_nt(high, low, values):
    vh, vl = halves(values)

    def dot(left, right):
        return lax.dot_general(left, right, (((1,), (1,)), ((), ())), preferred_element_type=f32)

    return dot(high, vh) + (dot(high, vl) + dot(low, vh))


def forward_y(s_ref, th_ref, tl_ref, out_ref, turned, mid, done):
    rows = s_ref.shape[0]
    count, lanes = th_ref.shape[0], th_ref.shape[1]
    for j in range(count):
        part = s_ref[:, j * lanes : (j + 1) * lanes].T
        turned[j * lanes : (j + 1) * lanes, :] = jnp.concatenate([part, part], 1)
    for a in range(count):
        part = turned[pl.ds(a, lanes, stride=count), :].T[:rows]
        mid[a] = dot_nn(part, th_ref[a], tl_ref[a])

    @pl.loop(0, CHUNKS)
    def _(chunk):
        @pl.loop(0, rows // CHUNKS // 8)
        def _(i):
            at = pl.ds(pl.multiple_of(chunk * (rows // CHUNKS) + i * 8, 8), 8)
            re = [mid[a, at, :lanes] for a in range(count)]
            im = [mid[a, at, lanes:] for a in range(count)]
            re, im = fft_list(re, im, -1.0)
            for d in range(count):
                out_ref[d, 0, at, :] = re[d]
                out_ref[d, 1, at, :] = im[d]

        done(chunk)


def inverse_y(w_ref, th_ref, tl_ref, out_ref, turned, mid, ready):
    rows = w_ref.shape[2]
    count, lanes = th_ref.shape[0], th_ref.shape[1]

    @pl.loop(0, CHUNKS)
    def _(chunk):
        ready(chunk)

        @pl.loop(0, rows // CHUNKS // 8)
        def _(i):
            at = pl.ds(pl.multiple_of(chunk * (rows // CHUNKS) + i * 8, 8), 8)
            re = [w_ref[d, 0, at, :] for d in range(count)]
            im = [w_ref[d, 1, at, :] for d in range(count)]
            re, im = fft_list(re, im, 1.0)
            for a in range(count):
                mid[a, at, :lanes] = re[a]
                mid[a, at, lanes:] = im[a]

    for a in range(count):
        part = dot_nt(th_ref[a], tl_ref[a], mid[a])
        turned[pl.ds(a, lanes, stride=count), :] = jnp.concatenate([part, part], 1)
    for j in range(count):
        part = turned[j * lanes : (j + 1) * lanes, :].T
        out_ref[:, j * lanes : (j + 1) * lanes] = part[:rows]


def middle(first, field, th_ref, tl_ref, hist_ref, k0_ref, k1_ref, s_ref, mid):
    lanes = field.shape[2]
    count = th_ref.shape[0]
    for a in range(count):
        at = pl.ds(a, 128, stride=count)
        part = jnp.concatenate([field[0, at, :].T, field[1, at, :].T], 1)
        mid[a] = dot_nn(part, th_ref[a], tl_ref[a])

    @pl.loop(0, lanes // 16)
    def _(i):
        for j in range(2):
            at = pl.ds(pl.multiple_of(i * 16 + 8 * j, 8), 8)
            both = pl.ds(pl.multiple_of(i * 16, 16), 16)
            re = [mid[a, at, :128] for a in range(count)]
            im = [mid[a, at, 128:] for a in range(count)]
            re, im = fft_list(re, im, -1.0)
            for k in range(count):
                cols = slice(k * 128, (k + 1) * 128)
                weight = k0_ref[both, cols].astype(f32)[8 * j : 8 * j + 8]
                if first:
                    s_ref[0, at, cols] = re[k]
                    s_ref[1, at, cols] = im[k]
                re[k] = weight * re[k] + hist_ref[0, at, cols]
                im[k] = weight * im[k] + hist_ref[1, at, cols]
                if not first:
                    weight = k1_ref[both, cols].astype(f32)[8 * j : 8 * j + 8]
                    re[k] = re[k] + weight * s_ref[0, at, cols]
                    im[k] = im[k] + weight * s_ref[1, at, cols]
            re, im = fft_list(re, im, 1.0)
            for a in range(count):
                mid[a, at, :128] = re[a]
                mid[a, at, 128:] = im[a]

    for a in range(count):
        at = pl.ds(a, 128, stride=count)
        part = dot_nt(th_ref[a], tl_ref[a], mid[a])
        field[0, at, :] = part[:128]
        field[1, at, :] = part[128:]


def field_kernel(first, *refs):
    rate_ref, yh, yl, xh, xl, kernel_ref = refs[:6]
    if first:
        modes_ref, far_ref, hist1, s_ref = refs[6:10]
        hist, k0, k1 = refs[10:13]
        rest = refs[13:]
    else:
        hist_in, s_in, far_ref = refs[6:9]
        hist, s_ref, k0, k1 = refs[9:13]
        rest = refs[13:]
    (strip, columns, field, returned, tile, turned, mid_y, mid_x,
     local_sem, pair_sem, send_sem, out_sem, in_sem) = rest
    devices, _, rows, lanes = columns.shape
    col_count = lax.axis_size("col")
    row_at, col_at = lax.axis_index("row"), lax.axis_index("col")
    me = row_at * col_count + col_at
    width = rate_ref.shape[1]

    def place(p):
        return {"row": p // col_count, "col": p % col_count}

    loads = [pltpu.make_async_copy(kernel_ref.at[0], k0, local_sem.at[0])]
    if not first:
        loads += [
            pltpu.make_async_copy(kernel_ref.at[1], k1, local_sem.at[1]),
            pltpu.make_async_copy(hist_in, hist, local_sem.at[2]),
            pltpu.make_async_copy(s_in, s_ref, local_sem.at[3]),
        ]
    for load in loads:
        load.start()

    barrier = pltpu.get_barrier_semaphore()

    @pl.loop(1, devices)
    def _(k):
        pl.semaphore_signal(barrier, 1, device_id=place((me + k) % devices))

    pl.semaphore_wait(barrier, devices - 1)

    other = 1 - col_at
    own_rows = pl.ds(pl.multiple_of(col_at * rows, rows), rows)
    pair_rows = pl.ds(pl.multiple_of(other * rows, rows), rows)
    own_cols = pl.ds(pl.multiple_of(col_at * width, width), width)
    pair_cols = pl.ds(pl.multiple_of(other * width, width), width)
    swap = pltpu.make_async_remote_copy(
        src_ref=rate_ref.at[pair_rows], dst_ref=strip.at[:, own_cols],
        send_sem=pair_sem.at[0], recv_sem=pair_sem.at[1], device_id=place(me + other - col_at),
    )
    swap.start()
    strip[:, own_cols] = rate_ref[own_rows, :]
    swap.wait()

    part_rows = rows // CHUNKS

    def forward_copy(chunk, p, source):
        at = pl.ds(pl.multiple_of(chunk * part_rows, part_rows), part_rows)
        to = pl.ds(pl.multiple_of(me * rows + chunk * part_rows, part_rows), part_rows)
        return pltpu.make_async_remote_copy(
            src_ref=columns.at[p, :, at, :], dst_ref=field.at[:, to, :],
            send_sem=send_sem.at[chunk, p], recv_sem=out_sem.at[chunk, source], device_id=place(p),
        )

    def backward_copy(chunk, p, source):
        at = pl.ds(pl.multiple_of(p * rows + chunk * part_rows, part_rows), part_rows)
        to = pl.ds(pl.multiple_of(chunk * part_rows, part_rows), part_rows)
        return pltpu.make_async_remote_copy(
            src_ref=field.at[:, at, :], dst_ref=returned.at[me, :, to, :],
            send_sem=send_sem.at[chunk, p], recv_sem=in_sem.at[chunk, source], device_id=place(p),
        )

    def send_columns(chunk):
        @pl.loop(1, devices)
        def _(k):
            forward_copy(chunk, (me + k) % devices, me).start()

    forward_y(strip, yh, yl, columns, turned, mid_y, send_columns)
    own = pl.ds(pl.multiple_of(me * rows, rows), rows)
    field[:, own, :] = columns[me]

    if first:
        history = functools.partial(history_body, hist, hist1)
        horizon, span, length = kernel_ref.shape
        pltpu.emit_pipeline(
            history,
            grid=(span // 16,),
            in_specs=[
                pl.BlockSpec((horizon, 16, length), lambda i: (0, i, 0)),
                pl.BlockSpec((horizon, 2, 16, length), lambda i: (0, 0, i, 0)),
            ],
        )(kernel_ref, modes_ref)

    for load in loads:
        load.wait()
    for chunk in range(CHUNKS):
        @pl.loop(1, devices)
        def _(k):
            p = (me + k) % devices
            forward_copy(chunk, p, p).wait_recv()

    for chunk in range(CHUNKS):
        @pl.loop(1, devices)
        def _(k):
            forward_copy(chunk, (me + k) % devices, me).wait_send()

    middle(first, field, xh, xl, hist, k0, k1, s_ref, mid_x)

    for chunk in range(CHUNKS):
        @pl.loop(1, devices)
        def _(k):
            backward_copy(chunk, (me + k) % devices, me).start()

    returned[me] = field[:, own, :]

    def receive(chunk):
        @pl.loop(1, devices)
        def _(k):
            p = (me + k) % devices
            backward_copy(chunk, p, p).wait_recv()

    inverse_y(returned, yh, yl, strip, turned, mid_y, receive)
    swap = pltpu.make_async_remote_copy(
        src_ref=strip.at[:, pair_cols], dst_ref=tile.at[own_rows],
        send_sem=pair_sem.at[2], recv_sem=pair_sem.at[3], device_id=place(me + other - col_at),
    )
    swap.start()
    far_ref[own_rows, :] = strip[:, own_cols]
    for chunk in range(CHUNKS):
        @pl.loop(1, devices)
        def _(k):
            backward_copy(chunk, (me + k) % devices, me).wait_send()

    swap.wait()
    far_ref[pair_rows, :] = tile[pair_rows, :]


def history_body(h0_ref, h1_ref, k_ref, m_ref):
    horizon, rows, length = k_ref.shape
    wide = 256
    at = pl.ds(pl.multiple_of(pl.program_id(0) * rows, rows), rows)

    @pl.loop(0, length // wide)
    def _(i):
        cols = pl.ds(pl.multiple_of(i * wide, wide), wide)
        acc = [[None, None], [None, None]]
        for h in range(horizon - 1):
            modes = [m_ref[h, c, :, cols].astype(f32) for c in range(2)]
            for step in range(2):
                if h + 1 + step < horizon:
                    weight = k_ref[h + 1 + step, :, cols].astype(f32)
                    for c in range(2):
                        term = weight * modes[c]
                        acc[step][c] = term if acc[step][c] is None else acc[step][c] + term
        for c in range(2):
            h0_ref[c, at, cols] = acc[0][c]
            h1_ref[c, at, cols] = acc[1][c]


def friction_kernel(far_ref, rate_ref, slip_ref, base_ref, now_ref, level_ref, trac_ref, slip_out, next_ref, rate_out):
    i = pl.program_id(0)

    def row(p):
        return level_ref[p, pl.ds(i, 1), :]

    static, dynamic, weakening, normal, initial = [row(p) for p in range(5)]
    rate = rate_ref[...]
    slip = slip_ref[...]
    strength = normal * (static - (static - dynamic) * jnp.minimum(slip / weakening, 1.0))
    trial = initial + far_ref[...] - damping * rate
    traction = jnp.minimum(jnp.maximum(trial, -strength), strength)
    trac_ref[...] = traction
    slip_out[...] = slip + jnp.abs(rate)
    following = base_ref[...] + courant * traction
    next_ref[...] = following
    rate_out[...] = following - now_ref[...]


def params(**more):
    return pltpu.CompilerParams(vmem_limit_bytes=VMEM_BYTES, **more)


def shape(*dims):
    return jax.ShapeDtypeStruct(dims, f32)


def field_call(first, rate, tables, kernel, *more):
    tile_rows, tile_cols = rate.shape
    _, span, length = kernel.shape
    col_count = lax.axis_size("col")
    devices = lax.axis_size("row") * col_count
    rows, width = tile_rows // col_count, tile_cols * col_count
    vmem, anywhere = pl.BlockSpec(memory_space=pltpu.VMEM), pl.BlockSpec(memory_space=pl.ANY)
    spectrum = (2, span, length)
    weights = [pltpu.VMEM((span, length), bf16)] * 2
    dma = pltpu.SemaphoreType.DMA
    common = [
        pltpu.VMEM((rows, width), f32),
        pltpu.VMEM((devices, 2, rows, span), f32),
        pltpu.VMEM((2, length, span), f32),
        pltpu.VMEM((devices, 2, rows, span), f32),
        pltpu.VMEM((tile_rows, tile_cols), f32),
        pltpu.VMEM((width, 2 * rows), f32),
        pltpu.VMEM((devices, rows, 2 * span), f32),
        pltpu.VMEM((length // 128, span, 256), f32),
        dma((4,)), dma((4,)), dma((CHUNKS, devices)), dma((CHUNKS, devices)), dma((CHUNKS, devices)),
    ]
    if first:
        scratch = [pltpu.VMEM(spectrum, f32)] + weights
        out = (shape(tile_rows, tile_cols), shape(*spectrum), shape(*spectrum))
        out_specs = (vmem,) * 3
    else:
        scratch = [pltpu.VMEM(spectrum, f32)] * 2 + weights
        out, out_specs = shape(tile_rows, tile_cols), vmem
    return pl.pallas_call(
        functools.partial(field_kernel, first),
        out_shape=out,
        in_specs=[vmem] * 5 + [anywhere] * (1 + len(more)),
        out_specs=out_specs,
        scratch_shapes=scratch + common,
        compiler_params=params(collective_id=0 if first else 1, has_side_effects=True),
    )(rate, *tables, kernel, *more)


def friction_step(far, rate, slip, base, now, levels):
    rows, cols = far.shape
    tile = pl.BlockSpec((BLOCK_CELLS, cols), lambda i: (i, 0))
    return pl.pallas_call(
        friction_kernel,
        grid=(rows // BLOCK_CELLS,),
        out_shape=(shape(rows, cols),) * 4,
        in_specs=[tile] * 5 + [pl.BlockSpec(levels.shape, lambda i: (0, 0, 0))],
        out_specs=(tile,) * 4,
        compiler_params=params(),
    )(far, rate, slip, base, now, levels)


def block_levels(region_ids, tables):
    mask = region_ids[None] == jnp.arange(tables[0].shape[0], dtype=jnp.int32)[:, None, None]
    picked = jnp.stack([jnp.sum(jnp.where(mask, t[:, None, None], 0.0), axis=0) for t in tables])
    return jnp.repeat(picked, BLOCK_CELLS, axis=2)


def with_halo(cells, sides, width):
    for axis, dim in sides:
        count = lax.axis_size(axis)
        head = lax.slice_in_dim(cells, 0, width, axis=dim)
        tail = lax.slice_in_dim(cells, cells.shape[dim] - width, cells.shape[dim], axis=dim)
        cells = jnp.concatenate(
            [
                lax.ppermute(tail, axis, [(i, (i + 1) % count) for i in range(count)]),
                cells,
                lax.ppermute(head, axis, [((i + 1) % count, i) for i in range(count)]),
            ],
            axis=dim,
        )
    return cells


def wave_base(current, previous):
    padded = with_halo(current, (("row", 1), ("col", 2)), 1)
    laplacian = (
        padded[:, 2:, 1:-1]
        + padded[:, :-2, 1:-1]
        + padded[:, 1:-1, 2:]
        + padded[:, 1:-1, :-2]
        - 4.0 * current
    )
    upper = jnp.concatenate([current[1:], jnp.zeros_like(current[:1])], 0)
    lower = jnp.concatenate([current[:1], current[:-1]], 0)
    return 2.0 * current - previous + courant * (laplacian + upper + lower - 2.0 * current)


def shards(
    wave_now,
    wave_before,
    fault_slip,
    region_ids,
    mode_history,
    wave_kernel,
    static_friction,
    dynamic_friction,
    weakening_slip,
    normal_stress,
    initial_stress,
):
    tile_rows, tile_cols = (wave_now.shape[1], wave_now.shape[2])
    col_count = lax.axis_size("col")
    devices = lax.axis_size("row") * col_count
    width = tile_cols * col_count
    span = wave_kernel.shape[1]
    length = wave_kernel.shape[2]
    rows = tile_rows // col_count
    if span != 128 or rows % (8 * CHUNKS) or col_count != 2 or length % 128:
        return general_shards(
            wave_now, wave_before, fault_slip, region_ids, mode_history, wave_kernel,
            static_friction, dynamic_friction, weakening_slip, normal_stress, initial_stress,
        )
    yh, yl = [jnp.asarray(t) for t in y_table(width, span)]
    xh, xl = [jnp.asarray(t) for t in x_table(length)]
    tables = (yh, yl, xh, xl)
    levels = block_levels(
        region_ids, (static_friction, dynamic_friction, weakening_slip, normal_stress, initial_stress)
    )
    current, previous, slip = wave_now, wave_before, fault_slip
    rate = current[0] - previous[0]
    for substep in range(SUBSTEPS):
        base = wave_base(current, previous)
        if substep == 0:
            far, hist, spectrum = field_call(True, rate, tables, wave_kernel, mode_history)
        else:
            far = field_call(False, rate, tables, wave_kernel, hist, spectrum)
        traction, slip, top, rate = friction_step(far, rate, slip, base[0], current[0], levels)
        previous = current
        current = jnp.stack([top, base[1]])
    return (current, slip, traction)


highest = lax.Precision.HIGHEST


def phase_table(first_count, second_count, modulus, sign):
    first = lax.broadcasted_iota(jnp.int32, (first_count, second_count), 0)
    second = lax.broadcasted_iota(jnp.int32, (first_count, second_count), 1)
    product = first * second % modulus
    angle = sign * 2.0 * math.pi / modulus * product.astype(jnp.float32)
    return (jnp.cos(angle), jnp.sin(angle))


def contract(form, left, right):
    return jnp.einsum(form, left, right, precision=highest, preferred_element_type=jnp.float32)


def complex_contract(form, left, right):
    real_part = contract(form, left[0], right[0]) - contract(form, left[1], right[1])
    imag_part = contract(form, left[0], right[1]) + contract(form, left[1], right[0])
    return (real_part, imag_part)


def complex_scale(pair, factor):
    return (pair[0] * factor[0] - pair[1] * factor[1], pair[0] * factor[1] + pair[1] * factor[0])


def forward_along_y(values):
    row_count, width = values.shape
    outer = 64
    inner = width // outer
    shaped = values.reshape(row_count, outer, inner)
    first_table = phase_table(outer, outer, outer, -1.0)
    sectioned = (
        contract("kn,rnm->rkm", first_table[0], shaped),
        contract("kn,rnm->rkm", first_table[1], shaped),
    )
    twiddle = phase_table(outer, inner, width, -1.0)
    sectioned = complex_scale(sectioned, (twiddle[0][None], twiddle[1][None]))
    second_table = phase_table(inner, inner, inner, -1.0)
    result = complex_contract("rkm,mq->qkr", sectioned, second_table)
    stacked = jnp.stack([result[0].reshape(width, row_count), result[1].reshape(width, row_count)])
    return stacked / math.sqrt(width)


def forward_along_x(pieces):
    blocks, span, block_rows = (pieces.shape[1], pieces.shape[2], pieces.shape[3])
    length = blocks * block_rows
    first_table = phase_table(blocks, blocks, blocks, -1.0)
    sectioned = complex_contract("ks,sji->kji", first_table, (pieces[0], pieces[1]))
    twiddle = phase_table(blocks, block_rows, length, -1.0)
    sectioned = complex_scale(sectioned, (twiddle[0][:, None, :], twiddle[1][:, None, :]))
    second_table = phase_table(block_rows, block_rows, block_rows, -1.0)
    result = complex_contract("kji,iq->jqk", sectioned, second_table)
    stacked = jnp.stack([result[0].reshape(span, length), result[1].reshape(span, length)])
    return stacked / math.sqrt(length)


def inverse_along_x(spectrum, blocks):
    span, length = (spectrum.shape[1], spectrum.shape[2])
    block_rows = length // blocks
    shaped = spectrum.reshape(2, span, block_rows, blocks)
    first_table = phase_table(block_rows, block_rows, block_rows, 1.0)
    sectioned = complex_contract("am,jmn->jan", first_table, (shaped[0], shaped[1]))
    twiddle = phase_table(block_rows, blocks, length, 1.0)
    sectioned = complex_scale(sectioned, (twiddle[0][None], twiddle[1][None]))
    second_table = phase_table(blocks, blocks, blocks, 1.0)
    result = complex_contract("jan,nb->bja", sectioned, second_table)
    stacked = jnp.stack(
        [result[0].reshape(blocks, span * block_rows), result[1].reshape(blocks, span * block_rows)]
    )
    return stacked / math.sqrt(length)


def inverse_along_y(spectrum):
    width, row_count = (spectrum.shape[1], spectrum.shape[2])
    outer = 64
    inner = width // outer
    shaped = spectrum.reshape(2, outer, inner, row_count)
    first_table = phase_table(outer, outer, outer, 1.0)
    sectioned = complex_contract("am,mnr->anr", first_table, (shaped[0], shaped[1]))
    twiddle = phase_table(outer, inner, width, 1.0)
    sectioned = complex_scale(sectioned, (twiddle[0][:, :, None], twiddle[1][:, :, None]))
    second_table = phase_table(inner, inner, inner, 1.0)
    real_part = contract("anr,nb->rba", sectioned[0], second_table[0]) - contract(
        "anr,nb->rba", sectioned[1], second_table[1]
    )
    return real_part.reshape(row_count, width) / math.sqrt(width)


def general_shards(
    wave_now,
    wave_before,
    fault_slip,
    region_ids,
    mode_history,
    wave_kernel,
    static_friction,
    dynamic_friction,
    weakening_slip,
    normal_stress,
    initial_stress,
):
    tile_rows, tile_cols = (wave_now.shape[1], wave_now.shape[2])
    row_count = lax.axis_size("row")
    col_count = lax.axis_size("col")
    col_index = lax.axis_index("col")
    blocks = row_count * col_count
    full_width = tile_cols * col_count
    span = full_width // blocks
    block_rows = region_ids.shape[0]
    block_cols = region_ids.shape[1]
    cell_ids = jnp.broadcast_to(
        region_ids[:, None, :, None], (block_rows, BLOCK_CELLS, block_cols, BLOCK_CELLS)
    ).reshape(tile_rows, tile_cols)
    region_mask = (
        cell_ids[None] == jnp.arange(static_friction.shape[0], dtype=jnp.int32)[:, None, None]
    )

    def lookup(table):
        return jnp.sum(jnp.where(region_mask, table[:, None, None], 0.0), axis=0)

    static_level = lookup(static_friction)
    dynamic_level = lookup(dynamic_friction)
    weakening = lookup(weakening_slip)
    normal_load = lookup(normal_stress)
    prestress = lookup(initial_stress)
    horizon = mode_history.shape[0]
    current = wave_now
    previous = wave_before
    slip = fault_slip
    traction = jnp.zeros_like(fault_slip)
    recent = []
    for substep in range(SUBSTEPS):
        slip_rate = current[0] - previous[0]
        padded = with_halo(current, (("row", 1), ("col", 2)), 1)
        whole_rows = lax.all_gather(slip_rate, "col", axis=1, tiled=True)
        columns = forward_along_y(whole_rows)
        own_part = lax.dynamic_index_in_dim(
            columns.reshape(2, row_count, col_count, -1), col_index, 2, keepdims=False
        )
        spread = lax.all_to_all(own_part, "row", split_axis=1, concat_axis=1, tiled=True)
        spectrum = forward_along_x(spread.reshape(2, row_count, span, tile_rows))
        recent.insert(0, spectrum)
        fresh = len(recent)
        wave_load = jnp.einsum(
            "hjk,hcjk->cjk",
            wave_kernel[fresh:],
            mode_history[: horizon - fresh],
            preferred_element_type=jnp.float32,
        )
        for offset in range(fresh):
            wave_load = wave_load + wave_kernel[offset].astype(jnp.float32)[None] * recent[offset]
        back_part = inverse_along_x(wave_load, row_count)
        returned = lax.all_to_all(back_part, "row", split_axis=1, concat_axis=1, tiled=True)
        joined = lax.all_gather(returned[:, :, None, :], "col", axis=2, tiled=True)
        whole_field = inverse_along_y(joined.reshape(2, full_width, tile_rows))
        far_field = lax.dynamic_slice_in_dim(whole_field, col_index * tile_cols, tile_cols, 1)
        trial_stress = prestress + far_field - damping * slip_rate
        strength = normal_load * (
            static_level - (static_level - dynamic_level) * jnp.minimum(slip / weakening, 1.0)
        )
        traction = jnp.clip(trial_stress, -strength, strength)
        slip = slip + jnp.abs(slip_rate)
        laplacian = (
            padded[:, 2:, 1:-1]
            + padded[:, :-2, 1:-1]
            + padded[:, 1:-1, 2:]
            + padded[:, 1:-1, :-2]
            - 4.0 * current
        )
        upper_cells = jnp.concatenate([current[1:], jnp.zeros_like(current[:1])], 0)
        lower_cells = jnp.concatenate([(current[0] + traction)[None], current[:-1]], 0)
        following = (
            2.0 * current
            - previous
            + courant * (laplacian + upper_cells + lower_cells - 2.0 * current)
        )
        previous = current
        current = following
    return (current, slip, traction)


def solution(mesh):
    return jax.shard_map(
        shards,
        mesh=mesh,
        in_specs=(
            P("groups", "row", "col"),
            P("groups", "row", "col"),
            P(("groups", "row"), "col"),
            P(("groups", "row"), "col"),
            P("groups", None, ("row", "col"), None),
            P(None, ("row", "col"), None),
            P(),
            P(),
            P(),
            P(),
            P(),
        ),
        out_specs=(
            P("groups", "row", "col"),
            P(("groups", "row"), "col"),
            P(("groups", "row"), "col"),
        ),
        check_vma=False,
    )
```
